32 devices in a mesh: groups: 2 (over x), ctx: 16 (over z, y, core).
Axes of the slice: x: 2, y: 2, z: 4, core: 2. Of those that a mesh axis runs over, the one named last changes fastest.
Arguments:
- queries: bfloat16 [4096, 4096], P(('groups', 'ctx')), parts along dimension 0, may hold values from -12 to 12
- keys: bfloat16 [4096, 512], P(('groups', 'ctx')), parts along dimension 0, may hold values from -9 to 9
- values: bfloat16 [4096, 512], P(('groups', 'ctx')), parts along dimension 0, may hold values from -6 to 6
- doc_lengths: int32 [32], P('groups'), parts along dimension 0, may hold values from 1 to 1024, 2048 in all
Outputs:
- attended: bfloat16 [4096, 4096], P(('groups', 'ctx')), parts along dimension 0
The draws below stay inside these ranges and needn't reach their ends.
There are 2 independent parts, one for each index of `groups`. The reference program is written for one: setup_inputs(seed, part) draws one part's arguments, and reference() takes and returns one part's arrays. A program takes and returns all parts, laid end to end along the dimension named above; each array names one. Nothing has to cross between parts.
Inputs may be any that keep to these rules, and one draw needn't show every extreme that they name: `doc_lengths`: the lengths sum to 2048, and the longest document has exactly 1024 tokens.
All inputs are finite; a program needn't handle non-finite values.
Results may differ from the reference program's by a relative error of at most 0.003.
Values may be sent and summed in bfloat16 or wider, within the bound.
No kernel may reach another device: no remote copies, remote signals or barrier semaphores. Data moves between devices by JAX's collectives and lax.ppermute only.
A program may use at most 128 MiB of HBM per device.

```python
import math
import jax
import jax.numpy as jnp
import numpy as np
from jax import lax

HEADS = 32
KV_HEADS = 4
HEAD_DIM = 128
NDOC = 16
WINDOW_TOKENS = 2048


def draw_queries(key, part):
    drawn_values = jax.random.normal(jax.random.fold_in(key, 11), (WINDOW_TOKENS, HEADS, HEAD_DIM), jnp.float32) * 2.0
    drawn_values = jnp.clip(drawn_values, -12.0, 12.0)
    return drawn_values.reshape(WINDOW_TOKENS, HEADS * HEAD_DIM).astype(jnp.bfloat16)


def draw_keys(key, part):
    drawn_values = jax.random.normal(jax.random.fold_in(key, 12), (WINDOW_TOKENS, KV_HEADS, HEAD_DIM), jnp.float32) * 1.5
    drawn_values = jnp.clip(drawn_values, -9.0, 9.0)
    return drawn_values.reshape(WINDOW_TOKENS, KV_HEADS * HEAD_DIM).astype(jnp.bfloat16)


def shard_levels(key, extent, pieces, smallest, largest):
    factor_of = 1.0
    for dim, shards_of in pieces:
        draws = jax.random.uniform(jax.random.fold_in(jax.random.fold_in(key, 6), dim), (shards_of,), jnp.float32, smallest / len(pieces), largest / len(pieces))
        factor_of = factor_of * jnp.repeat(jnp.exp(draws), extent[dim] // shards_of).reshape((-1,) + (1,) * (len(extent) - 1 - dim))
    return factor_of


def profile(amount, total, limit, slope):
    loads = [(1 << 20) // math.isqrt(grade ** slope) + 1 for grade in range(2, amount + 1)]
    spare, counts = total - limit - (amount - 1), [1] * (amount - 1)
    while spare > 0:
        free = [i for i in range(amount - 1) if counts[i] < limit]
        whole, budget = sum([loads[i] for i in free]), spare
        for i in free:
            addition = min(limit - counts[i], max(1, budget * loads[i] // whole), spare)
            counts[i] = counts[i] + addition
            spare = spare - addition
    return np.array([limit] + counts)


def ragged_sizes(key, number_of, total, limit, lean):
    if number_of == 2:
        one = jax.random.randint(key, (), max(1, total - limit), min(limit, total - 1) + 1)
        return jnp.stack([one, total - one])
    tallies = jnp.asarray(profile(number_of, total, limit, lean), jnp.int32)
    pairs = (number_of - 1) // 2
    giver, taker = tallies[1:1 + 2 * pairs:2], tallies[2:2 + 2 * pairs:2]
    slack = jnp.minimum(giver - 1, limit - taker)
    passed = jax.random.randint(jax.random.fold_in(key, 1), (pairs,), 0, 1 << 20) % (slack + 1)
    tallies = tallies.at[1:1 + 2 * pairs:2].set(giver - passed).at[2:2 + 2 * pairs:2].set(taker + passed)
    return tallies[jax.random.permutation(jax.random.fold_in(key, 2), number_of)]


def scatter_about(own_key, dims, scale, limit, cuts=(), kind=jnp.bfloat16):
    values = jax.random.normal(own_key, dims, jnp.float32) * scale
    if len(cuts) > 0:
        values = shard_levels(own_key, dims, cuts, -0.22, 0.18) * values
    return jnp.clip(values, min=-limit, max=limit).astype(kind)


def setup_inputs(seed: int = 0, part: int = 0) -> dict:
    key_list = jax.random.split(jax.random.key(seed), 5)
    part_splits = jax.random.split(jax.random.fold_in(key_list[4], part), 5)
    queries = draw_queries(jax.random.fold_in(jax.random.fold_in(key_list[4], part), 71), part)
    keys = draw_keys(jax.random.fold_in(jax.random.fold_in(key_list[4], part), 71), part)
    values = scatter_about(part_splits[2], (WINDOW_TOKENS, KV_HEADS * HEAD_DIM), 1.0, 6.0, ((0, 16),))
    doc_lengths = ragged_sizes(part_splits[3], NDOC, WINDOW_TOKENS, WINDOW_TOKENS // 2, 2).astype(jnp.int32)
    return dict(queries=queries, keys=keys, values=values, doc_lengths=doc_lengths)


negative_filler = -1e+30

def doc_index(positions, doc_ends):
    return lax.optimization_barrier(jnp.sum((doc_ends[None, :] <= positions[:, None]).astype(jnp.int32), axis=1))

def reference(queries, keys, values, doc_lengths):
    group_size = HEADS // KV_HEADS
    doc_ends = jnp.cumsum(doc_lengths).astype(jnp.int32)
    positions = jnp.arange(WINDOW_TOKENS, dtype=jnp.int32)
    doc_ids = doc_index(positions, doc_ends)
    key_wide = keys.reshape(WINDOW_TOKENS, KV_HEADS, HEAD_DIM).astype(jnp.float32)
    value_wide = values.reshape(WINDOW_TOKENS, KV_HEADS, HEAD_DIM).astype(jnp.float32)
    block_rows = math.gcd(WINDOW_TOKENS, 128)
    scale_factor = 1.0 / math.sqrt(HEAD_DIM)

    def single_block(block_start):
        query_block = lax.dynamic_slice_in_dim(queries, block_start, block_rows, 0)
        query_block = query_block.reshape(block_rows, KV_HEADS, group_size, HEAD_DIM).astype(jnp.float32)
        query_position = block_start + jnp.arange(block_rows, dtype=jnp.int32)
        query_doc = lax.dynamic_slice_in_dim(doc_ids, block_start, block_rows, 0)
        visible = (doc_ids[None, :] == query_doc[:, None]) & (positions[None, :] <= query_position[:, None])
        logit_scores = jnp.einsum('qhgd,khd->hgqk', query_block, key_wide) * scale_factor
        logit_scores = jnp.where(visible[None, None], logit_scores, negative_filler)
        row_max = lax.optimization_barrier(jnp.max(logit_scores, axis=3, keepdims=True))
        attention_weight = jnp.where(visible[None, None], jnp.exp(logit_scores - row_max), 0.0)
        denominator = lax.optimization_barrier(jnp.sum(attention_weight, axis=3))
        rounded = lax.optimization_barrier(attention_weight.astype(jnp.bfloat16)).astype(jnp.float32)
        summed = jnp.einsum('hgqk,khd->qhgd', rounded, value_wide)
        result = summed / jnp.transpose(denominator, (2, 0, 1))[..., None]
        return result.reshape(block_rows, HEADS * HEAD_DIM).astype(jnp.bfloat16)
    block_starts = jnp.arange(WINDOW_TOKENS // block_rows, dtype=jnp.int32) * block_rows
    blocks = lax.map(single_block, block_starts)
    return blocks.reshape(WINDOW_TOKENS, HEADS * HEAD_DIM)
```

```python
import functools
import math

import jax
import jax.numpy as jnp
from jax import lax
from jax.experimental import pallas as pl
from jax.experimental.pallas import tpu as pltpu
from jax.sharding import PartitionSpec as P

HEADS = 32
KV_HEADS = 4
HEAD_DIM = 128
GROUP = HEADS // KV_HEADS
NEG = -1e30
EXP2_SCALE = math.log2(math.e) / math.sqrt(HEAD_DIM)


def document_starts(doc_ref, position):
    start = jnp.zeros_like(position)
    end = jnp.int32(0)
    for d in range(doc_ref.shape[0]):
        end = end + doc_ref[d]
        start = jnp.where(position >= end, end, start)
    return start


def attend_kernel(first, last, offsets, picks, plane, *refs):
    n_pairs = max(max(p) for p in picks) + 1
    doc_ref, q_ref = refs[:2]
    kv_refs = refs[2 : 2 + 2 * n_pairs]
    rest = refs[2 + 2 * n_pairs :]
    if first:
        rest = (None, None) + rest
    acc_in, ml_in = rest[:2]
    rest = rest[2:]
    rows = q_ref.shape[0]
    me = lax.axis_index("ctx")
    chip, core = me // 2, me % 2
    odd = chip % 2 == 1
    lane = lax.broadcasted_iota(jnp.int32, (rows, rows), 1)
    position = me * rows + lax.broadcasted_iota(jnp.int32, (rows, rows), 0)
    start = document_starts(doc_ref, position)
    biases = []
    for offset in offsets:
        for other in (0, 1):
            block = 2 * (chip - offset) + (core if other == 0 else 1 - core)
            key = block * rows + lane
            biases.append(jnp.where((key >= start) & (key <= position), 0.0, NEG))
    bias = jnp.concatenate(biases, axis=1)
    keys = bias.shape[1]
    ones = jnp.ones((keys, HEAD_DIM), jnp.bfloat16)

    def columns(column):
        tiles = []
        for even_pick, odd_pick in picks:
            for other in (0, 1):
                at = pl.ds(pl.multiple_of(column * HEAD_DIM, HEAD_DIM), HEAD_DIM)
                tile = kv_refs[2 * even_pick + other][:, at]
                if odd_pick != even_pick:
                    tile = jnp.where(odd, kv_refs[2 * odd_pick + other][:, at], tile)
                tiles.append(tile)
        return jnp.concatenate(tiles, axis=0)

    def body(j, carry):
        key_tile = columns(j)
        value_tile = jnp.concatenate([columns(KV_HEADS + j), ones], axis=1)
        ml_new = jnp.zeros((rows, HEAD_DIM), jnp.float32)
        for g in range(GROUP):
            at = pl.ds(pl.multiple_of((j * GROUP + g) * HEAD_DIM, HEAD_DIM), HEAD_DIM)
            scores = lax.dot_general(
                q_ref[:, at], key_tile, (((1,), (1,)), ((), ())), preferred_element_type=jnp.float32
            )
            scores = scores + bias
            top = jnp.max(scores, axis=1, keepdims=True)
            if not first:
                top_before = ml_in[j][:, g : g + 1]
                total_before = ml_in[j][:, GROUP + g : GROUP + g + 1]
                top = jnp.maximum(top, top_before)
            weights = jnp.exp2((scores - top) * EXP2_SCALE).astype(jnp.bfloat16)
            both = jnp.dot(weights, value_tile, preferred_element_type=jnp.float32)
            acc, total = both[:, :HEAD_DIM], both[:, HEAD_DIM:]
            if not first:
                fade = jnp.exp2((top_before - top) * EXP2_SCALE)
                acc = acc + acc_in[:, at] * fade
                total = total + total_before * fade
            if last:
                rest[0][:, at] = (acc / total).astype(jnp.bfloat16)
            else:
                rest[0][:, at] = acc
                ml_new = jnp.where(lane == g, top, ml_new)
                ml_new = jnp.where(lane == GROUP + g, total, ml_new)
        if not last:
            rest[1][j] = ml_new
        return carry

    lax.fori_loop(0, KV_HEADS, body, 0)


def attend(doc_lengths, queries, pairs, offsets, picks, plane, state=None, last=True):
    rows = queries.shape[0]
    first = state is None
    operands = [doc_lengths, queries] + [block for pair in pairs for block in pair] + list(state or ())
    vmem = pl.BlockSpec(memory_space=pltpu.VMEM)
    in_specs = [pl.BlockSpec(memory_space=pltpu.SMEM)] + [vmem] * (len(operands) - 1)
    if last:
        out_shape = jax.ShapeDtypeStruct(queries.shape, jnp.bfloat16)
        out_specs = vmem
    else:
        out_shape = (
            jax.ShapeDtypeStruct(queries.shape, jnp.float32),
            jax.ShapeDtypeStruct((KV_HEADS, rows, HEAD_DIM), jnp.float32),
        )
        out_specs = (vmem, vmem)
    keys = 2 * rows * len(offsets)
    return pl.pallas_call(
        functools.partial(attend_kernel, first, last, offsets, picks, plane),
        out_shape=out_shape,
        in_specs=in_specs,
        out_specs=out_specs,
        compiler_params=pltpu.CompilerParams(vmem_limit_bytes=40 * 1024 * 1024),
        cost_estimate=pl.CostEstimate(
            flops=4 * rows * HEADS * HEAD_DIM * keys,
            bytes_accessed=queries.size * 4 + keys * 2 * KV_HEADS * HEAD_DIM * 2,
            transcendentals=rows * HEADS * keys,
        ),
    )(*operands)


def local(n, queries, keys, values, doc_lengths):
    plane = 4
    reach = n // 2 // plane

    def swap(x, bit):
        return lax.ppermute(x, "ctx", [(i, i ^ bit) for i in range(n)])

    def onward(x):
        return lax.ppermute(x, "ctx", [(i, (i + plane) % n) for i in range(n)])

    column = [jnp.concatenate([keys, values], axis=1)]
    for _ in range(reach):
        column.append(onward(column[-1]))
    across = [swap(x, 2) for x in column]
    column = [(x, swap(x, 1)) for x in column]
    across = [(x, swap(x, 1)) for x in across]

    early_pairs = column[:reach] + across[:reach]
    early_offsets, early_picks = [], []
    for d in range(reach):
        early_offsets.append(2 * d)
        early_picks.append((d, d))
        if d > 0:
            early_offsets.append(2 * d - 1)
            early_picks.append((reach + d, reach + d - 1))
    state = attend(doc_lengths, queries, early_pairs, early_offsets, early_picks, plane, last=False)
    late_pairs = [column[reach], across[reach], across[reach - 1]]
    return attend(
        doc_lengths, queries, late_pairs, [2 * reach - 1, 2 * reach], [(1, 2), (0, 0)], plane, state=state
    )


def solution(mesh):
    spec = P(("groups", "ctx"), None)
    return jax.shard_map(
        functools.partial(local, mesh.shape["ctx"]),
        mesh=mesh,
        in_specs=(spec, spec, spec, P("groups")),
        out_specs=spec,
        check_vma=False,
    )
```

```python
import functools
import math

import jax
import jax.numpy as jnp
from jax import lax
from jax.experimental import pallas as pl
from jax.experimental.pallas import tpu as pltpu
from jax.sharding import PartitionSpec as P

HEADS = 32
KV_HEADS = 4
HEAD_DIM = 128
GROUP = HEADS // KV_HEADS
NEG = -1e30
EXP2_SCALE = math.log2(math.e) / math.sqrt(HEAD_DIM)


def document_starts(doc_ref, position):
    start = jnp.zeros_like(position)
    end = jnp.int32(0)
    for d in range(doc_ref.shape[0]):
        end = end + doc_ref[d]
        start = jnp.where(position >= end, end, start)
    return start


def attend_kernel(first, last, blocks, *refs):
    n_blocks = len(blocks)
    doc_ref, q_ref = refs[:2]
    k_refs, v_refs = refs[2 : 2 + n_blocks], refs[2 + n_blocks : 2 + 2 * n_blocks]
    rest = refs[2 + 2 * n_blocks :]
    if not first:
        acc_in, top_in, total_in = rest[:3]
        rest = rest[3:]
    rows = q_ref.shape[0]
    me = lax.axis_index("ctx")
    plane, y, core = me // 4, me // 2 % 2, me % 2
    lane = lax.broadcasted_iota(jnp.int32, (rows, rows), 1)
    position = me * rows + lax.broadcasted_iota(jnp.int32, (rows, rows), 0)
    start = document_starts(doc_ref, position)
    biases = []
    for back, flip_y, flip_core in blocks:
        block = 4 * (plane - back) + 2 * (1 - y if flip_y else y) + (1 - core if flip_core else core)
        key = block * rows + lane
        biases.append(jnp.where((key >= start) & (key <= position), 0.0, NEG))
    bias = jnp.concatenate(biases, axis=1)
    keys = bias.shape[1]
    ones = jnp.ones((keys, HEAD_DIM), jnp.bfloat16)

    def head_columns(head):
        return pl.ds(pl.multiple_of(head * HEAD_DIM, HEAD_DIM), HEAD_DIM)

    def body(j, carry):
        at = head_columns(j)
        key_tile = jnp.concatenate([r[:, at] for r in k_refs], axis=0)
        value_tile = jnp.concatenate([r[:, at] for r in v_refs], axis=0)
        value_tile = jnp.concatenate([value_tile, ones], axis=1)
        for g in range(GROUP):
            at = head_columns(j * GROUP + g)
            scores = lax.dot_general(
                q_ref[:, at], key_tile, (((1,), (1,)), ((), ())), preferred_element_type=jnp.float32
            )
            scores = scores + bias
            top = jnp.broadcast_to(jnp.max(scores, axis=1, keepdims=True), (rows, HEAD_DIM))
            if not first:
                top_before = top_in[:, at]
                top = jnp.maximum(top, top_before)
            weights = jnp.concatenate(
                [jnp.exp2((scores[:, i : i + HEAD_DIM] - top) * EXP2_SCALE) for i in range(0, keys, HEAD_DIM)], axis=1
            )
            both = jnp.dot(weights.astype(jnp.bfloat16), value_tile, preferred_element_type=jnp.float32)
            acc, total = both[:, :HEAD_DIM], both[:, HEAD_DIM:]
            if not first:
                fade = jnp.exp2((top_before - top) * EXP2_SCALE)
                acc = acc + acc_in[:, at] * fade
                total = total + total_in[:, at] * fade
            if last:
                rest[0][:, at] = (acc / total).astype(jnp.bfloat16)
            else:
                rest[0][:, at] = acc
                rest[1][:, at] = top
                rest[2][:, at] = total
        return carry

    lax.fori_loop(0, KV_HEADS, body, 0)


def attend(doc_lengths, queries, blocks, state=None, last=False):
    rows = queries.shape[0]
    first = state is None
    operands = [doc_lengths, queries] + [kv[0] for kv in blocks.values()] + [kv[1] for kv in blocks.values()]
    operands += list(state or ())
    vmem = pl.BlockSpec(memory_space=pltpu.VMEM)
    in_specs = [pl.BlockSpec(memory_space=pltpu.SMEM)] + [vmem] * (len(operands) - 1)
    if last:
        out_shape, out_specs = jax.ShapeDtypeStruct(queries.shape, jnp.bfloat16), vmem
    else:
        out_shape, out_specs = (jax.ShapeDtypeStruct(queries.shape, jnp.float32),) * 3, (vmem,) * 3
    keys = rows * len(blocks)
    return pl.pallas_call(
        functools.partial(attend_kernel, first, last, tuple(blocks)),
        out_shape=out_shape,
        in_specs=in_specs,
        out_specs=out_specs,
        compiler_params=pltpu.CompilerParams(vmem_limit_bytes=40 * 1024 * 1024),
        cost_estimate=pl.CostEstimate(
            flops=4 * rows * HEADS * HEAD_DIM * keys,
            bytes_accessed=queries.size * 4 + keys * 2 * KV_HEADS * HEAD_DIM * 2,
            transcendentals=rows * HEADS * keys,
        ),
    )(*operands)


def local(n, queries, keys, values, doc_lengths):
    reach = n // 2 // 4

    def swap(kv, bit):
        return tuple(lax.ppermute(x, "ctx", [(i, i ^ bit) for i in range(n)]) for x in kv)

    def onward(kv):
        return tuple(lax.ppermute(x, "ctx", [(i, (i + 4) % n) for i in range(n)]) for x in kv)

    column = [(keys, values)]
    for _ in range(reach):
        column.append(onward(column[-1]))
    across = [swap(kv, 2) for kv in column]

    def with_core(z, y):
        kv = across[z] if y else column[z]
        return {(z, y, 0): kv, (z, y, 1): swap(kv, 1)}

    state = attend(doc_lengths, queries, with_core(0, 0) | with_core(0, 1) | with_core(1, 0))
    for z in range(1, reach):
        state = attend(doc_lengths, queries, with_core(z, 1) | with_core(z + 1, 0), state)
    return attend(doc_lengths, queries, with_core(reach, 1), state, last=True)


def solution(mesh):
    spec = P(("groups", "ctx"), None)
    return jax.shard_map(
        functools.partial(local, mesh.shape["ctx"]),
        mesh=mesh,
        in_specs=(spec, spec, spec, P("groups")),
        out_specs=spec,
        check_vma=False,
    )
```

```python
import functools
import math

import jax
import jax.numpy as jnp
from jax import lax
from jax.experimental import pallas as pl
from jax.experimental.pallas import tpu as pltpu
from jax.sharding import PartitionSpec as P

HEADS = 32
KV_HEADS = 4
HEAD_DIM = 128
GROUP = HEADS // KV_HEADS
NEG = -1e30
EXP2_SCALE = math.log2(math.e) / math.sqrt(HEAD_DIM)
VMEM = pl.BlockSpec(memory_space=pltpu.VMEM)
HBM = pl.BlockSpec(memory_space=pltpu.HBM)


def head_columns(head, count=1):
    return pl.ds(head * HEAD_DIM, count * HEAD_DIM)


def document_starts(doc_ref, position):
    start = jnp.zeros_like(position)
    end = jnp.int32(0)
    for d in range(doc_ref.shape[0]):
        end = end + doc_ref[d]
        start = jnp.where(position >= end, end, start)
    return start


def place():
    me = lax.axis_index("ctx")
    return me // 4, me // 2 % 2, me % 2


def update_heads(j, q_ref, key_tile, value_tile, bias, state, emit):
    rows, keys = bias.shape
    value_tile = jnp.concatenate([value_tile, jnp.ones((keys, HEAD_DIM), jnp.bfloat16)], axis=1)
    for g in range(GROUP):
        at = head_columns(j * GROUP + g)
        scores = lax.dot_general(
            q_ref[:, at], key_tile, (((1,), (1,)), ((), ())), preferred_element_type=jnp.float32
        )
        scores = scores + bias
        top = jnp.broadcast_to(jnp.max(scores, axis=1, keepdims=True), (rows, HEAD_DIM))
        if state is not None:
            top_before = state[1][:, at]
            top = jnp.maximum(top, top_before)
        weights = jnp.concatenate(
            [jnp.exp2((scores[:, i : i + HEAD_DIM] - top) * EXP2_SCALE) for i in range(0, keys, HEAD_DIM)], axis=1
        )
        both = jnp.dot(weights.astype(jnp.bfloat16), value_tile, preferred_element_type=jnp.float32)
        acc, total = both[:, :HEAD_DIM], both[:, HEAD_DIM:]
        if state is not None:
            fade = jnp.exp2((top_before - top) * EXP2_SCALE)
            acc = acc + state[0][:, at] * fade
            total = total + state[2][:, at] * fade
        emit(at, acc, top, total)


def position_in(block, rows):
    return block * rows + lax.broadcasted_iota(jnp.int32, (rows, rows), 1)


def pack_kernel(k_hbm, v_hbm, kv_ref, sems):
    half = k_hbm.shape[1]
    copies = [
        pltpu.make_async_copy(src, kv_ref.at[:, pl.ds(i * half, half)], sems.at[i])
        for i, src in enumerate((k_hbm, v_hbm))
    ]
    for copy in copies:
        copy.start()
    for copy in copies:
        copy.wait()


def pack(keys, values):
    rows, half = keys.shape
    return pl.pallas_call(
        pack_kernel,
        out_shape=jax.ShapeDtypeStruct((rows, 2 * half), keys.dtype),
        in_specs=[HBM] * 2,
        out_specs=VMEM,
        scratch_shapes=[pltpu.SemaphoreType.DMA((2,))],
        compiler_params=pltpu.CompilerParams(vmem_limit_bytes=1024 * 1024),
    )(*(pltpu.with_memory_space_constraint(x, pltpu.HBM) for x in (keys, values)))


def first_kernel(doc_hbm, q_hbm, own, sib, back, back_sib, acc, top, total, q_ref, start_ref, doc_ref, doc_sem, q_sems):
    rows = q_ref.shape[0]
    small = pltpu.make_async_copy(doc_hbm, doc_ref, doc_sem)
    width = GROUP * HEAD_DIM
    large = [
        pltpu.make_async_copy(
            q_hbm.at[:, pl.ds(j * width, width)], q_ref.at[:, pl.ds(j * width, width)], q_sems.at[j]
        )
        for j in range(KV_HEADS)
    ]
    for copy in [small] + large:
        copy.start()
    plane, y, core = place()
    chip = 2 * plane + y
    position = (2 * chip + core) * rows + lax.broadcasted_iota(jnp.int32, (rows, rows), 0)
    small.wait()
    start = document_starts(doc_ref, position)
    start_ref[...] = start
    blocks = [2 * c + other for c in (chip, chip - 2) for other in (core, 1 - core)]
    keys = jnp.concatenate([position_in(block, rows) for block in blocks], axis=1)
    start, position = (jnp.concatenate([x] * len(blocks), axis=1) for x in (start, position))
    bias = jnp.where((keys >= start) & (keys <= position), 0.0, NEG)

    def emit(at, *new):
        acc[:, at], top[:, at], total[:, at] = new

    for j in range(KV_HEADS):
        large[j].wait()
        key_tile, value_tile = (
            jnp.concatenate([x[:, head_columns(head)] for x in (own, sib, back, back_sib)], axis=0)
            for head in (j, KV_HEADS + j)
        )
        update_heads(j, q_ref, key_tile, value_tile, bias, None, emit)


def attend_first(doc_lengths, queries, *blocks):
    rows = queries.shape[0]
    wide = jax.ShapeDtypeStruct(queries.shape, jnp.float32)
    return pl.pallas_call(
        first_kernel,
        out_shape=(wide, wide, wide, queries, jax.ShapeDtypeStruct((rows, rows), jnp.int32)),
        in_specs=[HBM] * 2 + [VMEM] * len(blocks),
        out_specs=(VMEM,) * 5,
        scratch_shapes=[
            pltpu.SMEM(doc_lengths.shape, jnp.int32),
            pltpu.SemaphoreType.DMA,
            pltpu.SemaphoreType.DMA((KV_HEADS,)),
        ],
        compiler_params=pltpu.CompilerParams(vmem_limit_bytes=20 * 1024 * 1024),
        cost_estimate=cost(rows, len(blocks)),
    )(*(pltpu.with_memory_space_constraint(x, pltpu.HBM) for x in (doc_lengths, queries)), *blocks)


def next_kernel(last, offsets, start_ref, q_ref, *refs):
    n_blocks = 2 * len(offsets)
    kv_refs, state, rest = refs[:n_blocks], refs[n_blocks : n_blocks + 3], refs[n_blocks + 3 :]
    rows = q_ref.shape[0]
    plane, y, core = place()
    chip = 2 * plane + y
    position = (2 * chip + core) * rows + lax.broadcasted_iota(jnp.int32, (rows, rows), 0)
    start = start_ref[...]
    blocks = [2 * (chip - offset) + other for offset in offsets for other in (core, 1 - core)]
    keys = [position_in(block, rows) for block in blocks]
    bias = jnp.concatenate([jnp.where((key >= start) & (key <= position), 0.0, NEG) for key in keys], axis=1)

    def tile(head):
        return jnp.concatenate([x[:, head_columns(head)] for x in kv_refs], axis=0)

    if last:
        out_hbm, out_ref, sems = rest

        def emit(at, acc, top, total):
            out_ref[:, at] = (acc / total).astype(jnp.bfloat16)
    else:

        def emit(at, *new):
            rest[0][:, at], rest[1][:, at], rest[2][:, at] = new

    copies = []
    for j in range(KV_HEADS):
        update_heads(j, q_ref, tile(j), tile(KV_HEADS + j), bias, state, emit)
        if last:
            at = head_columns(j * GROUP, GROUP)
            copies.append(pltpu.make_async_copy(out_ref.at[:, at], out_hbm.at[:, at], sems.at[j]))
            copies[-1].start()
    for copy in copies:
        copy.wait()


def attend_next(start, queries, blocks, offsets, state, last=False):
    rows = queries.shape[0]
    wide = jax.ShapeDtypeStruct(queries.shape, jnp.float32)
    scratch = []
    if last:
        scratch = [pltpu.VMEM(queries.shape, queries.dtype), pltpu.SemaphoreType.DMA((KV_HEADS,))]
    return pl.pallas_call(
        functools.partial(next_kernel, last, offsets),
        out_shape=jax.ShapeDtypeStruct(queries.shape, queries.dtype) if last else (wide,) * 3,
        in_specs=[VMEM] * (2 + len(blocks) + 3),
        out_specs=HBM if last else (VMEM,) * 3,
        scratch_shapes=scratch,
        compiler_params=pltpu.CompilerParams(vmem_limit_bytes=20 * 1024 * 1024),
        cost_estimate=cost(rows, len(blocks)),
    )(start, queries, *blocks, *state)


def cost(rows, blocks):
    keys = rows * blocks
    return pl.CostEstimate(
        flops=4 * rows * HEADS * HEAD_DIM * keys * 10,
        bytes_accessed=rows * HEADS * HEAD_DIM * 8,
        transcendentals=rows * HEADS * keys,
    )


def local(n, queries, keys, values, doc_lengths):
    reach = n // 2 // 4

    def permute(block, target):
        return lax.ppermute(block, "ctx", [(i, target(i)) for i in range(n)])

    def swap(block, bit):
        return permute(block, lambda i: i ^ bit)

    def onward(block, hop):
        fixed = 4 * (hop - 1)
        return permute(block, lambda i: i if i < fixed else fixed + (i - fixed + 4) % (n - fixed))

    def after(block, state):
        return lax.optimization_barrier((block, state))[0]

    def pair(block):
        return block, swap(block, 1)

    even = lax.axis_index("ctx") // 2 % 2 == 0
    own = pack(keys, values)
    column = [own, onward(own, 1)]
    if reach > 1:
        column.append(onward(column[1], 2))
    across = [swap(jnp.where(even, own, column[1]), 2)]
    *state, q, start = attend_first(doc_lengths, queries, *pair(own), *pair(column[1]))
    for z in range(2, reach + 1):
        if z < reach:
            column.append(onward(after(column[z], state[0]), z + 1))
        across.append(swap(after(jnp.where(even, after(column[z - 1], across[-1]), column[z]), state[0]), 2))
        blocks = pair(column[z]) + pair(after(across[z - 2], state[0]))
        state = attend_next(start, q, blocks, (2 * z, 2 * z - 3), state)
    return attend_next(start, q, pair(after(across[-1], state[0])), (2 * reach - 1,), state, last=True)


def solution(mesh):
    spec = P(("groups", "ctx"), None)
    return jax.shard_map(
        functools.partial(local, mesh.shape["ctx"]),
        mesh=mesh,
        in_specs=(spec, spec, spec, P("groups")),
        out_specs=spec,
        check_vma=False,
    )
```

```python
import functools
import math

import jax
import jax.numpy as jnp
from jax import lax
from jax.experimental import pallas as pl
from jax.experimental.pallas import tpu as pltpu
from jax.sharding import PartitionSpec as P

HEADS = 32
KV_HEADS = 4
HEAD_DIM = 128
GROUP = HEADS // KV_HEADS
NEG = -1e30
EXP2_SCALE = math.log2(math.e) / math.sqrt(HEAD_DIM)
VMEM = pl.BlockSpec(memory_space=pltpu.VMEM)
HBM = pl.BlockSpec(memory_space=pltpu.HBM)


def head_columns(head, count=1):
    return pl.ds(head * HEAD_DIM, count * HEAD_DIM)


def document_starts(doc_ref, position):
    start = jnp.zeros_like(position)
    end = jnp.int32(0)
    for d in range(doc_ref.shape[0]):
        end = end + doc_ref[d]
        start = jnp.where(position >= end, end, start)
    return start


def place():
    me = lax.axis_index("ctx")
    return me // 4, me // 2 % 2, me % 2


def update_heads(j, q_ref, key_tile, value_tile, bias, state, emit):
    rows, keys = bias.shape
    value_tile = jnp.concatenate([value_tile, jnp.ones((keys, HEAD_DIM), jnp.bfloat16)], axis=1)
    for g in range(GROUP):
        at = head_columns(j * GROUP + g)
        scores = lax.dot_general(
            q_ref[:, at], key_tile, (((1,), (1,)), ((), ())), preferred_element_type=jnp.float32
        )
        scores = scores + bias
        top = jnp.broadcast_to(jnp.max(scores, axis=1, keepdims=True), (rows, HEAD_DIM))
        if state is not None:
            top_before = state[1][:, at]
            top = jnp.maximum(top, top_before)
        weights = jnp.concatenate(
            [jnp.exp2((scores[:, i : i + HEAD_DIM] - top) * EXP2_SCALE) for i in range(0, keys, HEAD_DIM)], axis=1
        )
        both = jnp.dot(weights.astype(jnp.bfloat16), value_tile, preferred_element_type=jnp.float32)
        acc, total = both[:, :HEAD_DIM], both[:, HEAD_DIM:]
        if state is not None:
            fade = jnp.exp2((top_before - top) * EXP2_SCALE)
            acc = acc + state[0][:, at] * fade
            total = total + state[2][:, at] * fade
        emit(at, acc, top, total)


def position_in(block, rows):
    return block * rows + lax.broadcasted_iota(jnp.int32, (rows, rows), 1)


def pack_kernel(k_hbm, v_hbm, kv_ref, sems):
    half = k_hbm.shape[1]
    copies = [
        pltpu.make_async_copy(src, kv_ref.at[:, pl.ds(i * half, half)], sems.at[i])
        for i, src in enumerate((k_hbm, v_hbm))
    ]
    for copy in copies:
        copy.start()
    for copy in copies:
        copy.wait()


def pack(keys, values):
    rows, half = keys.shape
    return pl.pallas_call(
        pack_kernel,
        out_shape=jax.ShapeDtypeStruct((rows, 2 * half), keys.dtype),
        in_specs=[HBM] * 2,
        out_specs=VMEM,
        scratch_shapes=[pltpu.SemaphoreType.DMA((2,))],
        compiler_params=pltpu.CompilerParams(vmem_limit_bytes=1024 * 1024),
    )(*(pltpu.with_memory_space_constraint(x, pltpu.HBM) for x in (keys, values)))


def first_kernel(doc_hbm, q_hbm, own, sib, back, back_sib, acc, top, total, q_ref, start_ref, doc_ref, doc_sem, q_sems):
    rows = q_ref.shape[0]
    small = pltpu.make_async_copy(doc_hbm, doc_ref, doc_sem)
    width = GROUP * HEAD_DIM
    large = [
        pltpu.make_async_copy(
            q_hbm.at[:, pl.ds(j * width, width)], q_ref.at[:, pl.ds(j * width, width)], q_sems.at[j]
        )
        for j in range(KV_HEADS)
    ]
    for copy in [small] + large:
        copy.start()
    plane, y, core = place()
    chip = 2 * plane + y
    position = (2 * chip + core) * rows + lax.broadcasted_iota(jnp.int32, (rows, rows), 0)
    small.wait()
    start = document_starts(doc_ref, position)
    start_ref[...] = start
    blocks = [2 * c + other for c in (chip, chip - 2) for other in (core, 1 - core)]
    keys = jnp.concatenate([position_in(block, rows) for block in blocks], axis=1)
    start, position = (jnp.concatenate([x] * len(blocks), axis=1) for x in (start, position))
    bias = jnp.where((keys >= start) & (keys <= position), 0.0, NEG)

    def emit(at, *new):
        acc[:, at], top[:, at], total[:, at] = new

    for j in range(KV_HEADS):
        large[j].wait()
        key_tile, value_tile = (
            jnp.concatenate([x[:, head_columns(head)] for x in (own, sib, back, back_sib)], axis=0)
            for head in (j, KV_HEADS + j)
        )
        update_heads(j, q_ref, key_tile, value_tile, bias, None, emit)


def attend_first(doc_lengths, queries, *blocks):
    rows = queries.shape[0]
    wide = jax.ShapeDtypeStruct(queries.shape, jnp.float32)
    return pl.pallas_call(
        first_kernel,
        out_shape=(wide, wide, wide, queries, jax.ShapeDtypeStruct((rows, rows), jnp.int32)),
        in_specs=[HBM] * 2 + [VMEM] * len(blocks),
        out_specs=(VMEM,) * 5,
        scratch_shapes=[
            pltpu.SMEM(doc_lengths.shape, jnp.int32),
            pltpu.SemaphoreType.DMA,
            pltpu.SemaphoreType.DMA((KV_HEADS,)),
        ],
        compiler_params=pltpu.CompilerParams(vmem_limit_bytes=20 * 1024 * 1024),
        cost_estimate=cost(rows, len(blocks)),
    )(*(pltpu.with_memory_space_constraint(x, pltpu.HBM) for x in (doc_lengths, queries)), *blocks)


def next_kernel(last, offsets, start_ref, q_ref, *refs):
    n_blocks = 2 * len(offsets)
    kv_refs, state, rest = refs[:n_blocks], refs[n_blocks : n_blocks + 3], refs[n_blocks + 3 :]
    rows = q_ref.shape[0]
    plane, y, core = place()
    chip = 2 * plane + y
    position = (2 * chip + core) * rows + lax.broadcasted_iota(jnp.int32, (rows, rows), 0)
    start = start_ref[...]
    blocks = [2 * (chip - offset) + other for offset in offsets for other in (core, 1 - core)]
    keys = [position_in(block, rows) for block in blocks]
    bias = jnp.concatenate([jnp.where((key >= start) & (key <= position), 0.0, NEG) for key in keys], axis=1)

    def tile(head):
        return jnp.concatenate([x[:, head_columns(head)] for x in kv_refs], axis=0)

    if last:
        out_hbm, out_ref, sems = rest

        def emit(at, acc, top, total):
            out_ref[:, at] = (acc / total).astype(jnp.bfloat16)
    else:

        def emit(at, *new):
            rest[0][:, at], rest[1][:, at], rest[2][:, at] = new

    copies = []
    for j in range(KV_HEADS):
        update_heads(j, q_ref, tile(j), tile(KV_HEADS + j), bias, state, emit)
        if last:
            at = head_columns(j * GROUP, GROUP)
            copies.append(pltpu.make_async_copy(out_ref.at[:, at], out_hbm.at[:, at], sems.at[j]))
            copies[-1].start()
    for copy in copies:
        copy.wait()


def attend_next(start, queries, blocks, offsets, state, last=False):
    rows = queries.shape[0]
    wide = jax.ShapeDtypeStruct(queries.shape, jnp.float32)
    scratch = []
    if last:
        scratch = [pltpu.VMEM(queries.shape, queries.dtype), pltpu.SemaphoreType.DMA((KV_HEADS,))]
    return pl.pallas_call(
        functools.partial(next_kernel, last, offsets),
        out_shape=jax.ShapeDtypeStruct(queries.shape, queries.dtype) if last else (wide,) * 3,
        in_specs=[VMEM] * (2 + len(blocks) + 3),
        out_specs=HBM if last else (VMEM,) * 3,
        scratch_shapes=scratch,
        compiler_params=pltpu.CompilerParams(vmem_limit_bytes=20 * 1024 * 1024),
        cost_estimate=cost(rows, len(blocks)),
    )(start, queries, *blocks, *state)


def cost(rows, blocks):
    keys = rows * blocks
    return pl.CostEstimate(
        flops=4 * rows * HEADS * HEAD_DIM * keys * 10,
        bytes_accessed=rows * HEADS * HEAD_DIM * 8,
        transcendentals=rows * HEADS * keys,
    )


def local(n, queries, keys, values, doc_lengths):
    reach = n // 2 // 4

    def permute(block, target):
        return lax.ppermute(block, "ctx", [(i, target(i)) for i in range(n)])

    def swap(block, bit):
        return permute(block, lambda i: i ^ bit)

    def onward(block, step, hop):
        fixed = 4 * (hop - 1)
        return permute(block, lambda i: i ^ 1 if i < fixed else fixed + (i - fixed + step) % (n - fixed))

    def after(block, other):
        return lax.optimization_barrier((block, other))[0]

    def pair(block):
        return block, swap(block, 1)

    even = lax.axis_index("ctx") // 2 % 2 == 0
    own = pack(keys, values)
    back = onward(own, 4, 1)
    far = [(onward(back, 4, 2), onward(back, 2, 2))] if reach > 1 else []
    back_pair = pair(back)
    across = swap(jnp.where(even, own, after(back, back_pair[1])), 2)
    *state, q, start = attend_first(doc_lengths, queries, *pair(own), *back_pair)
    blocks, offsets = (across,), (1,)
    for z in range(2, reach + 1):
        here, beside = (after(block, state[0]) for block in far[-1])
        blocks, offsets = blocks + (here, beside), offsets + (2 * z, 2 * z - 1)
        if z < reach:
            far.append((onward(here, 4, z + 1), onward(here, 2, z + 1)))
            state = attend_next(start, q, [x for block in blocks for x in pair(block)], offsets, state)
            blocks, offsets = (), ()
    blocks = [x for block in blocks for x in pair(after(block, state[0]))]
    return attend_next(start, q, blocks, offsets, state, last=True)


def solution(mesh):
    spec = P(("groups", "ctx"), None)
    return jax.shard_map(
        functools.partial(local, mesh.shape["ctx"]),
        mesh=mesh,
        in_specs=(spec, spec, spec, P("groups")),
        out_specs=spec,
        check_vma=False,
    )
```

```python
import functools
import math

import jax
import jax.numpy as jnp
from jax import lax
from jax.experimental import pallas as pl
from jax.experimental.pallas import tpu as pltpu
from jax.sharding import PartitionSpec as P

HEADS = 32
KV_HEADS = 4
HEAD_DIM = 128
GROUP = HEADS // KV_HEADS
NEG = -1e30
EXP2_SCALE = math.log2(math.e) / math.sqrt(HEAD_DIM)
VMEM = pl.BlockSpec(memory_space=pltpu.VMEM)
HBM = pl.BlockSpec(memory_space=pltpu.HBM)


def head_columns(head, count=1):
    return pl.ds(head * HEAD_DIM, count * HEAD_DIM)


def document_starts(doc_ref, position):
    start = jnp.zeros_like(position)
    end = jnp.int32(0)
    for d in range(doc_ref.shape[0]):
        end = end + doc_ref[d]
        start = jnp.where(position >= end, end, start)
    return start


def place():
    me = lax.axis_index("ctx")
    return me // 4, me // 2 % 2, me % 2


def update_heads(j, q_ref, key_tile, value_tile, bias, state, emit):
    rows, keys = bias.shape
    value_tile = jnp.concatenate([value_tile, jnp.ones((keys, HEAD_DIM), jnp.bfloat16)], axis=1)
    for g in range(GROUP):
        at = head_columns(j * GROUP + g)
        scores = lax.dot_general(
            q_ref[:, at], key_tile, (((1,), (1,)), ((), ())), preferred_element_type=jnp.float32
        )
        scores = scores + bias
        top = jnp.broadcast_to(jnp.max(scores, axis=1, keepdims=True), (rows, HEAD_DIM))
        if state is not None:
            top_before = state[1][:, at]
            top = jnp.maximum(top, top_before)
        weights = jnp.concatenate(
            [jnp.exp2((scores[:, i : i + HEAD_DIM] - top) * EXP2_SCALE) for i in range(0, keys, HEAD_DIM)], axis=1
        )
        both = jnp.dot(weights.astype(jnp.bfloat16), value_tile, preferred_element_type=jnp.float32)
        acc, total = both[:, :HEAD_DIM], both[:, HEAD_DIM:]
        if state is not None:
            fade = jnp.exp2((top_before - top) * EXP2_SCALE)
            acc = acc + state[0][:, at] * fade
            total = total + state[2][:, at] * fade
        emit(at, acc, top, total)


def position_in(block, rows):
    return block * rows + lax.broadcasted_iota(jnp.int32, (rows, rows), 1)


def pack_kernel(k_hbm, v_hbm, kv_ref, sems):
    half = k_hbm.shape[1]
    copies = [
        pltpu.make_async_copy(src, kv_ref.at[:, pl.ds(i * half, half)], sems.at[i])
        for i, src in enumerate((k_hbm, v_hbm))
    ]
    for copy in copies:
        copy.start()
    for copy in copies:
        copy.wait()


def pack(keys, values):
    rows, half = keys.shape
    return pl.pallas_call(
        pack_kernel,
        out_shape=jax.ShapeDtypeStruct((rows, 2 * half), keys.dtype),
        in_specs=[HBM] * 2,
        out_specs=VMEM,
        scratch_shapes=[pltpu.SemaphoreType.DMA((2,))],
        compiler_params=pltpu.CompilerParams(vmem_limit_bytes=1024 * 1024),
    )(*(pltpu.with_memory_space_constraint(x, pltpu.HBM) for x in (keys, values)))


def first_kernel(doc_hbm, q_hbm, own, sib, back, back_sib, acc, top, total, q_ref, start_ref, doc_ref, doc_sem, q_sems):
    rows = q_ref.shape[0]
    small = pltpu.make_async_copy(doc_hbm, doc_ref, doc_sem)
    width = GROUP * HEAD_DIM
    large = [
        pltpu.make_async_copy(
            q_hbm.at[:, pl.ds(j * width, width)], q_ref.at[:, pl.ds(j * width, width)], q_sems.at[j]
        )
        for j in range(KV_HEADS)
    ]
    for copy in [small] + large:
        copy.start()
    plane, y, core = place()
    chip = 2 * plane + y
    position = (2 * chip + core) * rows + lax.broadcasted_iota(jnp.int32, (rows, rows), 0)
    small.wait()
    start = document_starts(doc_ref, position)
    start_ref[...] = start
    blocks = [2 * c + other for c in (chip, chip - 2) for other in (core, 1 - core)]
    keys = jnp.concatenate([position_in(block, rows) for block in blocks], axis=1)
    start, position = (jnp.concatenate([x] * len(blocks), axis=1) for x in (start, position))
    bias = jnp.where((keys >= start) & (keys <= position), 0.0, NEG)

    def emit(at, *new):
        acc[:, at], top[:, at], total[:, at] = new

    for j in range(KV_HEADS):
        large[j].wait()
        key_tile, value_tile = (
            jnp.concatenate([x[:, head_columns(head)] for x in (own, sib, back, back_sib)], axis=0)
            for head in (j, KV_HEADS + j)
        )
        update_heads(j, q_ref, key_tile, value_tile, bias, None, emit)


def attend_first(doc_lengths, queries, *blocks):
    rows = queries.shape[0]
    wide = jax.ShapeDtypeStruct(queries.shape, jnp.float32)
    return pl.pallas_call(
        first_kernel,
        out_shape=(wide, wide, wide, queries, jax.ShapeDtypeStruct((rows, rows), jnp.int32)),
        in_specs=[HBM] * 2 + [VMEM] * len(blocks),
        out_specs=(VMEM,) * 5,
        scratch_shapes=[
            pltpu.SMEM(doc_lengths.shape, jnp.int32),
            pltpu.SemaphoreType.DMA,
            pltpu.SemaphoreType.DMA((KV_HEADS,)),
        ],
        compiler_params=pltpu.CompilerParams(vmem_limit_bytes=20 * 1024 * 1024),
        cost_estimate=cost(rows, len(blocks)),
    )(*(pltpu.with_memory_space_constraint(x, pltpu.HBM) for x in (doc_lengths, queries)), *blocks)


def next_kernel(last, places, start_ref, q_ref, *refs):
    n_blocks = len(places)
    kv_refs, state, rest = refs[:n_blocks], refs[n_blocks : n_blocks + 3], refs[n_blocks + 3 :]
    rows = q_ref.shape[0]
    plane, y, core = place()
    chip = 2 * plane + y
    position = (2 * chip + core) * rows + lax.broadcasted_iota(jnp.int32, (rows, rows), 0)
    start = start_ref[...]
    first_start = jnp.min(start[:8])

    if last:
        out_hbm, out_ref, sems = rest

        def emit(at, acc, top, total):
            out_ref[:, at] = (acc / total).astype(jnp.bfloat16)
    else:

        def emit(at, *new):
            rest[0][:, at], rest[1][:, at], rest[2][:, at] = new

    def out_copy(j):
        at = head_columns(j * GROUP, GROUP)
        return pltpu.make_async_copy(out_ref.at[:, at], out_hbm.at[:, at], sems.at[j])

    def update(used):
        if used:
            keys = [position_in(2 * (chip - places[b][0]) + (core ^ places[b][1]), rows) for b in used]
            bias = [jnp.where((key >= start) & (key <= position), 0.0, NEG) for key in keys]
            bias = jnp.concatenate(bias, axis=1)
        for j in range(KV_HEADS):
            if used:
                key_tile, value_tile = (
                    jnp.concatenate([kv_refs[b][:, head_columns(head)] for b in used], axis=0)
                    for head in (j, KV_HEADS + j)
                )
                update_heads(j, q_ref, key_tile, value_tile, bias, state, emit)
            else:
                for g in range(GROUP):
                    at = head_columns(j * GROUP + g)
                    emit(at, *(x[:, at] for x in state))
            if last:
                out_copy(j).start()

    every = list(range(n_blocks))
    near = [b for b in every if places[b][0] == min(places)[0]]
    further = [offset for offset, _ in places if offset > min(places)[0]]

    def seen(offset):
        return (2 * (chip - offset) + 2) * rows > first_start

    seen_near = seen(min(places)[0])
    pl.when(jnp.logical_not(seen_near))(lambda: update([]))
    if further and len(near) > 1:
        seen_all = seen(min(further))
        pl.when(seen_near & jnp.logical_not(seen_all))(lambda: update(near))
        pl.when(seen_all)(lambda: update(every))
    else:
        pl.when(seen_near)(lambda: update(every))

    if last:
        for j in range(KV_HEADS):
            out_copy(j).wait()


def attend_next(start, queries, blocks, places, state, last=False):
    rows = queries.shape[0]
    wide = jax.ShapeDtypeStruct(queries.shape, jnp.float32)
    scratch = []
    if last:
        scratch = [pltpu.VMEM(queries.shape, queries.dtype), pltpu.SemaphoreType.DMA((KV_HEADS,))]
    return pl.pallas_call(
        functools.partial(next_kernel, last, places),
        out_shape=jax.ShapeDtypeStruct(queries.shape, queries.dtype) if last else (wide,) * 3,
        in_specs=[VMEM] * (2 + len(blocks) + 3),
        out_specs=HBM if last else (VMEM,) * 3,
        scratch_shapes=scratch,
        compiler_params=pltpu.CompilerParams(vmem_limit_bytes=20 * 1024 * 1024),
        cost_estimate=cost(rows, len(blocks)),
    )(start, queries, *blocks, *state)


def cost(rows, blocks):
    keys = rows * blocks
    return pl.CostEstimate(
        flops=4 * rows * HEADS * HEAD_DIM * keys * 10,
        bytes_accessed=rows * HEADS * HEAD_DIM * 8,
        transcendentals=rows * HEADS * keys,
    )


def local(n, queries, keys, values, doc_lengths):
    reach = n // 2 // 4

    def permute(block, target):
        return lax.ppermute(block, "ctx", [(i, target(i)) for i in range(n)])

    def swap(block, bit):
        return permute(block, lambda i: i ^ bit)

    def onward(block, step, hop):
        fixed = 4 * (hop - 1)
        return permute(block, lambda i: i ^ 1 if i < fixed else fixed + (i - fixed + step) % (n - fixed))

    def after(block, other):
        return lax.optimization_barrier((block, other))[0]

    def pair(block):
        return block, swap(block, 1)

    own = pack(keys, values)
    beside = swap(own, 2)
    back = onward(own, 4, 1)
    back_beside = permute(beside, lambda i: i ^ 1 if i // 2 % 2 else (i + 4) % n)
    far = (onward(back, 4, 2), onward(back, 2, 2)) if reach > 1 else ()
    *state, q, start = attend_first(doc_lengths, queries, *pair(own), *pair(back))
    back_beside, beside, far = after((back_beside, beside, far), state[0])
    even = lax.axis_index("ctx") // 2 % 2 == 0
    blocks, places = pair(jnp.where(even, back_beside, beside)), ((1, 0), (1, 1))
    for z in range(2, reach + 1):
        here, other = far, tuple(swap(block, 1) for block in far)
        if z < reach:
            far = after((onward(far[0], 4, z + 1), onward(far[0], 2, z + 1)), state[0])
        state = attend_next(start, q, here, ((2 * z, 0), (2 * z - 1, 0)), state)
        blocks, places = blocks + other, places + ((2 * z, 1), (2 * z - 1, 1))
        if z < reach:
            state = attend_next(start, q, blocks, places, state)
            blocks, places = (), ()
    return attend_next(start, q, blocks, places, state, last=True)


def solution(mesh):
    spec = P(("groups", "ctx"), None)
    return jax.shard_map(
        functools.partial(local, mesh.shape["ctx"]),
        mesh=mesh,
        in_specs=(spec, spec, spec, P("groups")),
        out_specs=spec,
        check_vma=False,
    )
```

```python
import functools
import math

import jax
import jax.numpy as jnp
from jax import lax
from jax.experimental import pallas as pl
from jax.experimental.pallas import tpu as pltpu
from jax.sharding import PartitionSpec as P

HEADS = 32
KV_HEADS = 4
HEAD_DIM = 128
GROUP = HEADS // KV_HEADS
NEG = -1e30
EXP2_SCALE = math.log2(math.e) / math.sqrt(HEAD_DIM)
VMEM = pl.BlockSpec(memory_space=pltpu.VMEM)
HBM = pl.BlockSpec(memory_space=pltpu.HBM)


def head_columns(head, count=1):
    return pl.ds(head * HEAD_DIM, count * HEAD_DIM)


def document_starts(doc_ref, position):
    start = jnp.zeros_like(position)
    end = jnp.int32(0)
    for d in range(doc_ref.shape[0]):
        end = end + doc_ref[d]
        start = jnp.where(position >= end, end, start)
    return start


def place():
    me = lax.axis_index("ctx")
    return me // 4, me // 2 % 2, me % 2


def update_heads(j, q_ref, key_tile, value_tile, bias, state, emit):
    rows, keys = bias.shape
    value_tile = jnp.concatenate([value_tile, jnp.ones((keys, HEAD_DIM), jnp.bfloat16)], axis=1)
    for g in range(GROUP):
        at = head_columns(j * GROUP + g)
        scores = lax.dot_general(
            q_ref[:, at], key_tile, (((1,), (1,)), ((), ())), preferred_element_type=jnp.float32
        )
        scores = scores + bias
        top = jnp.broadcast_to(jnp.max(scores, axis=1, keepdims=True), (rows, HEAD_DIM))
        if state is not None:
            top_before = state[1][:, at]
            top = jnp.maximum(top, top_before)
        weights = jnp.concatenate(
            [jnp.exp2((scores[:, i : i + HEAD_DIM] - top) * EXP2_SCALE) for i in range(0, keys, HEAD_DIM)], axis=1
        )
        both = jnp.dot(weights.astype(jnp.bfloat16), value_tile, preferred_element_type=jnp.float32)
        acc, total = both[:, :HEAD_DIM], both[:, HEAD_DIM:]
        if state is not None:
            fade = jnp.exp2((top_before - top) * EXP2_SCALE)
            acc = acc + state[0][:, at] * fade
            total = total + state[2][:, at] * fade
        emit(at, acc, top, total)


def position_in(block, rows):
    return block * rows + lax.broadcasted_iota(jnp.int32, (rows, rows), 1)


def pack_kernel(k_hbm, v_hbm, kv_ref, sems):
    half = k_hbm.shape[1]
    copies = [
        pltpu.make_async_copy(src, kv_ref.at[:, pl.ds(i * half, half)], sems.at[i])
        for i, src in enumerate((k_hbm, v_hbm))
    ]
    for copy in copies:
        copy.start()
    for copy in copies:
        copy.wait()


def pack(keys, values):
    rows, half = keys.shape
    return pl.pallas_call(
        pack_kernel,
        out_shape=jax.ShapeDtypeStruct((rows, 2 * half), keys.dtype),
        in_specs=[HBM] * 2,
        out_specs=VMEM,
        scratch_shapes=[pltpu.SemaphoreType.DMA((2,))],
        compiler_params=pltpu.CompilerParams(vmem_limit_bytes=1024 * 1024),
    )(*(pltpu.with_memory_space_constraint(x, pltpu.HBM) for x in (keys, values)))


def first_kernel(doc_hbm, q_hbm, own, sib, back, back_sib, acc, top, total, q_ref, start_ref, doc_ref, doc_sem, q_sems):
    rows = q_ref.shape[0]
    small = pltpu.make_async_copy(doc_hbm, doc_ref, doc_sem)
    width = GROUP * HEAD_DIM
    large = [
        pltpu.make_async_copy(
            q_hbm.at[:, pl.ds(j * width, width)], q_ref.at[:, pl.ds(j * width, width)], q_sems.at[j]
        )
        for j in range(KV_HEADS)
    ]
    for copy in [small] + large:
        copy.start()
    plane, y, core = place()
    chip = 2 * plane + y
    position = (2 * chip + core) * rows + lax.broadcasted_iota(jnp.int32, (rows, rows), 0)
    small.wait()
    start = document_starts(doc_ref, position)
    start_ref[...] = start
    blocks = [2 * c + other for c in (chip, chip - 2) for other in (core, 1 - core)]
    keys = jnp.concatenate([position_in(block, rows) for block in blocks], axis=1)
    start, position = (jnp.concatenate([x] * len(blocks), axis=1) for x in (start, position))
    bias = jnp.where((keys >= start) & (keys <= position), 0.0, NEG)

    def emit(at, *new):
        acc[:, at], top[:, at], total[:, at] = new

    for j in range(KV_HEADS):
        large[j].wait()
        key_tile, value_tile = (
            jnp.concatenate([x[:, head_columns(head)] for x in (own, sib, back, back_sib)], axis=0)
            for head in (j, KV_HEADS + j)
        )
        update_heads(j, q_ref, key_tile, value_tile, bias, None, emit)


def attend_first(doc_lengths, queries, *blocks):
    rows = queries.shape[0]
    wide = jax.ShapeDtypeStruct(queries.shape, jnp.float32)
    return pl.pallas_call(
        first_kernel,
        out_shape=(wide, wide, wide, queries, jax.ShapeDtypeStruct((rows, rows), jnp.int32)),
        in_specs=[HBM] * 2 + [VMEM] * len(blocks),
        out_specs=(VMEM,) * 5,
        scratch_shapes=[
            pltpu.SMEM(doc_lengths.shape, jnp.int32),
            pltpu.SemaphoreType.DMA,
            pltpu.SemaphoreType.DMA((KV_HEADS,)),
        ],
        compiler_params=pltpu.CompilerParams(vmem_limit_bytes=20 * 1024 * 1024),
        cost_estimate=cost(rows, len(blocks)),
    )(*(pltpu.with_memory_space_constraint(x, pltpu.HBM) for x in (doc_lengths, queries)), *blocks)


def next_kernel(last, places, start_ref, q_ref, *refs):
    n_blocks = len(places)
    kv_refs, state, rest = refs[:n_blocks], refs[n_blocks : n_blocks + 3], refs[n_blocks + 3 :]
    rows = q_ref.shape[0]
    plane, y, core = place()
    chip = 2 * plane + y
    position = (2 * chip + core) * rows + lax.broadcasted_iota(jnp.int32, (rows, rows), 0)
    start = start_ref[...]
    first_start = jnp.min(start[:8])

    if last:
        out_hbm, out_ref, sems = rest

        def emit(at, acc, top, total):
            out_ref[:, at] = (acc / total).astype(jnp.bfloat16)
    else:

        def emit(at, *new):
            rest[0][:, at], rest[1][:, at], rest[2][:, at] = new

    def out_copy(j):
        at = head_columns(j * (GROUP // 2), GROUP // 2)
        return pltpu.make_async_copy(out_ref.at[:, at], out_hbm.at[:, at], sems.at[j])

    def update(used):
        if used:
            keys = [position_in(2 * (chip - places[b][0]) + (core ^ places[b][1]), rows) for b in used]
            bias = [jnp.where((key >= start) & (key <= position), 0.0, NEG) for key in keys]
            bias = jnp.concatenate(bias, axis=1)
        for j in range(KV_HEADS):
            if used:
                key_tile, value_tile = (
                    jnp.concatenate([kv_refs[b][:, head_columns(head)] for b in used], axis=0)
                    for head in (j, KV_HEADS + j)
                )
                update_heads(j, q_ref, key_tile, value_tile, bias, state, emit)
            else:
                for g in range(GROUP):
                    at = head_columns(j * GROUP + g)
                    emit(at, *(x[:, at] for x in state))
            if last:
                out_copy(2 * j).start()
                out_copy(2 * j + 1).start()

    every = list(range(n_blocks))
    nearest, furthest = (pick(offset for offset, _ in places) for pick in (min, max))
    near = [b for b in every if places[b][0] < furthest]

    def seen(offset):
        return (2 * (chip - offset) + 2) * rows > first_start

    pl.when(jnp.logical_not(seen(nearest)))(lambda: update([]))
    if near and len(near) % 2 == 0:
        pl.when(seen(nearest) & jnp.logical_not(seen(furthest)))(lambda: update(near))
        pl.when(seen(furthest))(lambda: update(every))
    else:
        pl.when(seen(nearest))(lambda: update(every))

    if last:
        for j in range(2 * KV_HEADS):
            out_copy(j).wait()


def attend_next(start, queries, blocks, places, state, last=False):
    rows = queries.shape[0]
    wide = jax.ShapeDtypeStruct(queries.shape, jnp.float32)
    scratch = []
    if last:
        scratch = [pltpu.VMEM(queries.shape, queries.dtype), pltpu.SemaphoreType.DMA((2 * KV_HEADS,))]
    return pl.pallas_call(
        functools.partial(next_kernel, last, places),
        out_shape=jax.ShapeDtypeStruct(queries.shape, queries.dtype) if last else (wide,) * 3,
        in_specs=[VMEM] * (2 + len(blocks) + 3),
        out_specs=HBM if last else (VMEM,) * 3,
        scratch_shapes=scratch,
        compiler_params=pltpu.CompilerParams(vmem_limit_bytes=20 * 1024 * 1024),
        cost_estimate=cost(rows, len(blocks)),
    )(start, queries, *blocks, *state)


def cost(rows, blocks):
    keys = rows * blocks
    return pl.CostEstimate(
        flops=4 * rows * HEADS * HEAD_DIM * keys * 10,
        bytes_accessed=rows * HEADS * HEAD_DIM * 8,
        transcendentals=rows * HEADS * keys,
    )


def local(n, queries, keys, values, doc_lengths):
    reach = n // 2 // 4

    def permute(block, target):
        return lax.ppermute(block, "ctx", [(i, target(i)) for i in range(n)])

    def swap(block, bit):
        return permute(block, lambda i: i ^ bit)

    def onward(block, step, hop):
        fixed = 4 * (hop - 1)
        return permute(block, lambda i: i ^ 1 if i < fixed else fixed + (i - fixed + step) % (n - fixed))

    def after(block, other):
        return lax.optimization_barrier((block, other))[0]

    def pair(block):
        return block, swap(block, 1)

    own = pack(keys, values)
    beside = swap(own, 2)
    back = onward(own, 4, 1)
    back_beside = permute(beside, lambda i: i ^ 1 if i // 2 % 2 else (i + 4) % n)
    far = (onward(back, 4, 2), onward(back, 2, 2)) if reach > 1 else ()
    *state, q, start = attend_first(doc_lengths, queries, *pair(own), *pair(back))
    back_beside, beside, far = after((back_beside, beside, far), state[0])
    even = lax.axis_index("ctx") // 2 % 2 == 0
    across = jnp.where(even, back_beside, beside)
    blocks, places = (across,), (1,)
    for z in range(2, reach + 1):
        here, there = far
        if z < reach:
            far = after((onward(here, 4, z + 1), onward(here, 2, z + 1)), state[0])
        blocks, places = (there,) + blocks, (2 * z - 1,) + places
        other = tuple(swap(block, 1) for block in blocks)
        if len(blocks) == 2:
            state = attend_next(start, q, blocks, tuple((offset, 0) for offset in places), state)
            blocks, places = (), ()
        blocks = blocks + other + pair(here)
        places = tuple((offset, 0) for offset in places) + tuple((offset, 1) for offset in (2 * z - 1, 1)[: len(other)])
        places = places + ((2 * z, 0), (2 * z, 1))
        if z < reach:
            state = attend_next(start, q, blocks, places, state)
            blocks, places = (), ()
    return attend_next(start, q, blocks, places, state, last=True)


def solution(mesh):
    spec = P(("groups", "ctx"), None)
    return jax.shard_map(
        functools.partial(local, mesh.shape["ctx"]),
        mesh=mesh,
        in_specs=(spec, spec, spec, P("groups")),
        out_specs=spec,
        check_vma=False,
    )
```

```python
import functools
import math

import jax
import jax.numpy as jnp
from jax import lax
from jax.experimental import pallas as pl
from jax.experimental.pallas import tpu as pltpu
from jax.sharding import PartitionSpec as P

HEADS = 32
KV_HEADS = 4
HEAD_DIM = 128
GROUP = HEADS // KV_HEADS
NEG = -1e30
EXP2_SCALE = math.log2(math.e) / math.sqrt(HEAD_DIM)
VMEM = pl.BlockSpec(memory_space=pltpu.VMEM)
HBM = pl.BlockSpec(memory_space=pltpu.HBM)


def head_columns(head, count=1):
    return pl.ds(head * HEAD_DIM, count * HEAD_DIM)


def document_starts(doc_ref, position):
    start = jnp.zeros_like(position)
    end = jnp.int32(0)
    for d in range(doc_ref.shape[0]):
        end = end + doc_ref[d]
        start = jnp.where(position >= end, end, start)
    return start


def place():
    me = lax.axis_index("ctx")
    return me // 4, me // 2 % 2, me % 2


def update_heads(j, q_ref, key_tile, value_tile, bias, state, emit):
    rows, keys = bias.shape
    value_tile = jnp.concatenate([value_tile, jnp.ones((keys, HEAD_DIM), jnp.bfloat16)], axis=1)
    for g in range(GROUP):
        at = head_columns(j * GROUP + g)
        scores = lax.dot_general(
            q_ref[:, at], key_tile, (((1,), (1,)), ((), ())), preferred_element_type=jnp.float32
        )
        scores = scores + bias
        top = jnp.broadcast_to(jnp.max(scores, axis=1, keepdims=True), (rows, HEAD_DIM))
        if state is not None:
            top_before = state[1][:, at]
            top = jnp.maximum(top, top_before)
        weights = jnp.concatenate(
            [jnp.exp2((scores[:, i : i + HEAD_DIM] - top) * EXP2_SCALE) for i in range(0, keys, HEAD_DIM)], axis=1
        )
        both = jnp.dot(weights.astype(jnp.bfloat16), value_tile, preferred_element_type=jnp.float32)
        acc, total = both[:, :HEAD_DIM], both[:, HEAD_DIM:]
        if state is not None:
            fade = jnp.exp2((top_before - top) * EXP2_SCALE)
            acc = acc + state[0][:, at] * fade
            total = total + state[2][:, at] * fade
        emit(at, acc, top, total)


def position_in(block, rows):
    return block * rows + lax.broadcasted_iota(jnp.int32, (rows, rows), 1)


def pack_kernel(k_hbm, v_hbm, kv_ref, sems):
    half = k_hbm.shape[1]
    copies = [
        pltpu.make_async_copy(src, kv_ref.at[:, pl.ds(i * half, half)], sems.at[i])
        for i, src in enumerate((k_hbm, v_hbm))
    ]
    for copy in copies:
        copy.start()
    for copy in copies:
        copy.wait()


def pack(keys, values):
    rows, half = keys.shape
    return pl.pallas_call(
        pack_kernel,
        out_shape=jax.ShapeDtypeStruct((rows, 2 * half), keys.dtype),
        in_specs=[HBM] * 2,
        out_specs=VMEM,
        scratch_shapes=[pltpu.SemaphoreType.DMA((2,))],
        compiler_params=pltpu.CompilerParams(vmem_limit_bytes=1024 * 1024),
    )(*(pltpu.with_memory_space_constraint(x, pltpu.HBM) for x in (keys, values)))


def first_kernel(doc_hbm, q_hbm, own, sib, back, back_sib, acc, top, total, q_ref, start_ref, doc_ref, doc_sem, q_sems):
    rows = q_ref.shape[0]
    small = pltpu.make_async_copy(doc_hbm, doc_ref, doc_sem)
    width = GROUP * HEAD_DIM
    large = [
        pltpu.make_async_copy(
            q_hbm.at[:, pl.ds(j * width, width)], q_ref.at[:, pl.ds(j * width, width)], q_sems.at[j]
        )
        for j in range(KV_HEADS)
    ]
    for copy in [small] + large:
        copy.start()
    plane, y, core = place()
    chip = 2 * plane + y
    position = (2 * chip + core) * rows + lax.broadcasted_iota(jnp.int32, (rows, rows), 0)
    small.wait()
    start = document_starts(doc_ref, position)
    start_ref[...] = start
    blocks = [2 * c + other for c in (chip, chip - 2) for other in (core, 1 - core)]
    keys = jnp.concatenate([position_in(block, rows) for block in blocks], axis=1)
    start, position = (jnp.concatenate([x] * len(blocks), axis=1) for x in (start, position))
    bias = jnp.where((keys >= start) & (keys <= position), 0.0, NEG)

    def emit(at, *new):
        acc[:, at], top[:, at], total[:, at] = new

    for j in range(KV_HEADS):
        large[j].wait()
        key_tile, value_tile = (
            jnp.concatenate([x[:, head_columns(head)] for x in (own, sib, back, back_sib)], axis=0)
            for head in (j, KV_HEADS + j)
        )
        update_heads(j, q_ref, key_tile, value_tile, bias, None, emit)


def attend_first(doc_lengths, queries, *blocks):
    rows = queries.shape[0]
    wide = jax.ShapeDtypeStruct(queries.shape, jnp.float32)
    return pl.pallas_call(
        first_kernel,
        out_shape=(wide, wide, wide, queries, jax.ShapeDtypeStruct((rows, rows), jnp.int32)),
        in_specs=[HBM] * 2 + [VMEM] * len(blocks),
        out_specs=(VMEM,) * 5,
        scratch_shapes=[
            pltpu.SMEM(doc_lengths.shape, jnp.int32),
            pltpu.SemaphoreType.DMA,
            pltpu.SemaphoreType.DMA((KV_HEADS,)),
        ],
        compiler_params=pltpu.CompilerParams(vmem_limit_bytes=20 * 1024 * 1024),
        cost_estimate=cost(rows, len(blocks)),
    )(*(pltpu.with_memory_space_constraint(x, pltpu.HBM) for x in (doc_lengths, queries)), *blocks)


def next_kernel(last, places, start_ref, q_ref, *refs):
    n_blocks = len(places)
    kv_refs, state, rest = refs[:n_blocks], refs[n_blocks : n_blocks + 3], refs[n_blocks + 3 :]
    rows = q_ref.shape[0]
    plane, y, core = place()
    chip = 2 * plane + y
    position = (2 * chip + core) * rows + lax.broadcasted_iota(jnp.int32, (rows, rows), 0)
    start = start_ref[...]
    first_start = jnp.min(start[:8])

    if last:
        out_hbm, out_ref, sems = rest

        def emit(at, acc, top, total):
            out_ref[:, at] = (acc / total).astype(jnp.bfloat16)
    else:

        def emit(at, *new):
            rest[0][:, at], rest[1][:, at], rest[2][:, at] = new

    def out_copy(j):
        at = head_columns(j * (GROUP // 2), GROUP // 2)
        return pltpu.make_async_copy(out_ref.at[:, at], out_hbm.at[:, at], sems.at[j])

    def update(used):
        if used:
            keys = [position_in(2 * (chip - places[b][0]) + (core ^ places[b][1]), rows) for b in used]
            bias = [jnp.where((key >= start) & (key <= position), 0.0, NEG) for key in keys]
            bias = jnp.concatenate(bias, axis=1)
        for j in range(KV_HEADS):
            if used:
                key_tile, value_tile = (
                    jnp.concatenate([kv_refs[b][:, head_columns(head)] for b in used], axis=0)
                    for head in (j, KV_HEADS + j)
                )
                update_heads(j, q_ref, key_tile, value_tile, bias, state, emit)
            else:
                for g in range(GROUP):
                    at = head_columns(j * GROUP + g)
                    emit(at, *(x[:, at] for x in state))
            if last:
                out_copy(2 * j).start()
                out_copy(2 * j + 1).start()

    every = list(range(n_blocks))
    nearest, furthest = (pick(offset for offset, _ in places) for pick in (min, max))
    near = [b for b in every if places[b][0] < furthest]

    def seen(offset):
        return (2 * (chip - offset) + 2) * rows > first_start

    pl.when(jnp.logical_not(seen(nearest)))(lambda: update([]))
    if near and len(near) % 2 == 0:
        pl.when(seen(nearest) & jnp.logical_not(seen(furthest)))(lambda: update(near))
        pl.when(seen(furthest))(lambda: update(every))
    else:
        pl.when(seen(nearest))(lambda: update(every))

    if last:
        for j in range(2 * KV_HEADS):
            out_copy(j).wait()


def attend_next(start, queries, blocks, places, state, last=False):
    rows = queries.shape[0]
    wide = jax.ShapeDtypeStruct(queries.shape, jnp.float32)
    scratch = []
    if last:
        scratch = [pltpu.VMEM(queries.shape, queries.dtype), pltpu.SemaphoreType.DMA((2 * KV_HEADS,))]
    return pl.pallas_call(
        functools.partial(next_kernel, last, places),
        out_shape=jax.ShapeDtypeStruct(queries.shape, queries.dtype) if last else (wide,) * 3,
        in_specs=[VMEM] * (2 + len(blocks) + 3),
        out_specs=HBM if last else (VMEM,) * 3,
        scratch_shapes=scratch,
        compiler_params=pltpu.CompilerParams(vmem_limit_bytes=20 * 1024 * 1024),
        cost_estimate=cost(rows, len(blocks)),
    )(start, queries, *blocks, *state)


def cost(rows, blocks):
    keys = rows * blocks
    return pl.CostEstimate(
        flops=4 * rows * HEADS * HEAD_DIM * keys * 10,
        bytes_accessed=rows * HEADS * HEAD_DIM * 8,
        transcendentals=rows * HEADS * keys,
    )


def local(n, queries, keys, values, doc_lengths):
    reach = n // 2 // 4

    def permute(block, target):
        return lax.ppermute(block, "ctx", [(i, target(i)) for i in range(n)])

    def swap(block, bit):
        return permute(block, lambda i: i ^ bit)

    def onward(block, step, hop):
        fixed = 4 * (hop - 1) - 2 * (step % 4)
        return permute(block, lambda i: i ^ 1 if i < fixed else fixed + (i - fixed + step) % (n - fixed))

    def after(block, other):
        return lax.optimization_barrier((block, other))[0]

    def pair(block):
        return block, swap(block, 1)

    own = pack(keys, values)
    beside = swap(own, 2)
    back = onward(own, 4, 1)
    back_beside = permute(beside, lambda i: i ^ 1 if i // 2 % 2 else (i + 4) % n)
    far = (onward(after(back, swap(beside, 1)), 4, 2), onward(back, 2, 2)) if reach > 1 else ()
    *state, q, start = attend_first(doc_lengths, queries, *pair(own), *pair(back))
    back_beside, beside, far = after((back_beside, beside, far), state[0])
    even = lax.axis_index("ctx") // 2 % 2 == 0
    across = jnp.where(even, back_beside, beside)
    blocks, places = (across,), (1,)
    for z in range(2, reach + 1):
        here, there = far
        if z < reach:
            far = after((onward(here, 4, z + 1), onward(here, 2, z + 1)), state[0])
        blocks, places = (there,) + blocks, (2 * z - 1,) + places
        other = tuple(swap(block, 1) for block in blocks)
        if len(blocks) == 2:
            state = attend_next(start, q, blocks, tuple((offset, 0) for offset in places), state)
            blocks, places = (), ()
        blocks = blocks + other + pair(here)
        places = tuple((offset, 0) for offset in places) + tuple((offset, 1) for offset in (2 * z - 1, 1)[: len(other)])
        places = places + ((2 * z, 0), (2 * z, 1))
        if z < reach:
            state = attend_next(start, q, blocks, places, state)
            blocks, places = (), ()
    return attend_next(start, q, blocks, places, state, last=True)


def solution(mesh):
    spec = P(("groups", "ctx"), None)
    return jax.shard_map(
        functools.partial(local, mesh.shape["ctx"]),
        mesh=mesh,
        in_specs=(spec, spec, spec, P("groups")),
        out_specs=spec,
        check_vma=False,
    )
```

```python
import functools
import math

import jax
import jax.numpy as jnp
from jax import lax
from jax.experimental import pallas as pl
from jax.experimental.pallas import tpu as pltpu
from jax.sharding import PartitionSpec as P

HEADS = 32
KV_HEADS = 4
HEAD_DIM = 128
GROUP = HEADS // KV_HEADS
NEG = -1e30
EXP2_SCALE = math.log2(math.e) / math.sqrt(HEAD_DIM)
VMEM = pl.BlockSpec(memory_space=pltpu.VMEM)
HBM = pl.BlockSpec(memory_space=pltpu.HBM)


def head_columns(head, count=1):
    return pl.ds(head * HEAD_DIM, count * HEAD_DIM)


def document_starts(doc_ref, position):
    start = jnp.zeros_like(position)
    end = jnp.int32(0)
    for d in range(doc_ref.shape[0]):
        end = end + doc_ref[d]
        start = jnp.where(position >= end, end, start)
    return start


def place():
    me = lax.axis_index("ctx")
    return me // 4, me // 2 % 2, me % 2


def update_heads(j, q_ref, key_tile, value_tile, bias, state, emit):
    rows, keys = bias.shape
    value_tile = jnp.concatenate([value_tile, jnp.ones((keys, HEAD_DIM), jnp.bfloat16)], axis=1)
    for g in range(GROUP):
        at = head_columns(j * GROUP + g)
        scores = lax.dot_general(
            q_ref[:, at], key_tile, (((1,), (1,)), ((), ())), preferred_element_type=jnp.float32
        )
        scores = scores + bias
        top = jnp.broadcast_to(jnp.max(scores, axis=1, keepdims=True), (rows, HEAD_DIM))
        if state is not None:
            top_before = state[1][:, at]
            top = jnp.maximum(top, top_before)
        weights = jnp.concatenate(
            [jnp.exp2((scores[:, i : i + HEAD_DIM] - top) * EXP2_SCALE) for i in range(0, keys, HEAD_DIM)], axis=1
        )
        both = jnp.dot(weights.astype(jnp.bfloat16), value_tile, preferred_element_type=jnp.float32)
        acc, total = both[:, :HEAD_DIM], both[:, HEAD_DIM:]
        if state is not None:
            fade = jnp.exp2((top_before - top) * EXP2_SCALE)
            acc = acc + state[0][:, at] * fade
            total = total + state[2][:, at] * fade
        emit(at, acc, top, total)


def position_in(block, rows):
    return block * rows + lax.broadcasted_iota(jnp.int32, (rows, rows), 1)


def pack_kernel(k_hbm, v_hbm, kv_ref, sems):
    half = k_hbm.shape[1]
    copies = [
        pltpu.make_async_copy(src, kv_ref.at[:, pl.ds(i * half, half)], sems.at[i])
        for i, src in enumerate((k_hbm, v_hbm))
    ]
    for copy in copies:
        copy.start()
    for copy in copies:
        copy.wait()


def pack(keys, values):
    rows, half = keys.shape
    return pl.pallas_call(
        pack_kernel,
        out_shape=jax.ShapeDtypeStruct((rows, 2 * half), keys.dtype),
        in_specs=[HBM] * 2,
        out_specs=VMEM,
        scratch_shapes=[pltpu.SemaphoreType.DMA((2,))],
        compiler_params=pltpu.CompilerParams(vmem_limit_bytes=1024 * 1024),
    )(*(pltpu.with_memory_space_constraint(x, pltpu.HBM) for x in (keys, values)))


def first_kernel(doc_hbm, q_hbm, own, sib, back, back_sib, acc, top, total, q_ref, start_ref, doc_ref, doc_sem, q_sems):
    rows = q_ref.shape[0]
    small = pltpu.make_async_copy(doc_hbm, doc_ref, doc_sem)
    width = GROUP * HEAD_DIM
    large = [
        pltpu.make_async_copy(
            q_hbm.at[:, pl.ds(j * width, width)], q_ref.at[:, pl.ds(j * width, width)], q_sems.at[j]
        )
        for j in range(KV_HEADS)
    ]
    for copy in [small] + large:
        copy.start()
    plane, y, core = place()
    chip = 2 * plane + y
    position = (2 * chip + core) * rows + lax.broadcasted_iota(jnp.int32, (rows, rows), 0)
    small.wait()
    start = document_starts(doc_ref, position)
    start_ref[...] = start
    blocks = [2 * c + other for c in (chip, chip - 2) for other in (core, 1 - core)]
    keys = jnp.concatenate([position_in(block, rows) for block in blocks], axis=1)
    start, position = (jnp.concatenate([x] * len(blocks), axis=1) for x in (start, position))
    bias = jnp.where((keys >= start) & (keys <= position), 0.0, NEG)

    def emit(at, *new):
        acc[:, at], top[:, at], total[:, at] = new

    for j in range(KV_HEADS):
        large[j].wait()
        key_tile, value_tile = (
            jnp.concatenate([x[:, head_columns(head)] for x in (own, sib, back, back_sib)], axis=0)
            for head in (j, KV_HEADS + j)
        )
        update_heads(j, q_ref, key_tile, value_tile, bias, None, emit)


def attend_first(doc_lengths, queries, *blocks):
    rows = queries.shape[0]
    wide = jax.ShapeDtypeStruct(queries.shape, jnp.float32)
    return pl.pallas_call(
        first_kernel,
        out_shape=(wide, wide, wide, queries, jax.ShapeDtypeStruct((rows, rows), jnp.int32)),
        in_specs=[HBM] * 2 + [VMEM] * len(blocks),
        out_specs=(VMEM,) * 5,
        scratch_shapes=[
            pltpu.SMEM(doc_lengths.shape, jnp.int32),
            pltpu.SemaphoreType.DMA,
            pltpu.SemaphoreType.DMA((KV_HEADS,)),
        ],
        compiler_params=pltpu.CompilerParams(vmem_limit_bytes=20 * 1024 * 1024),
        cost_estimate=cost(rows, len(blocks)),
    )(*(pltpu.with_memory_space_constraint(x, pltpu.HBM) for x in (doc_lengths, queries)), *blocks)


def next_kernel(last, places, start_ref, q_ref, *refs):
    n_blocks = len(places)
    kv_refs, state, rest = refs[:n_blocks], refs[n_blocks : n_blocks + 3], refs[n_blocks + 3 :]
    rows = q_ref.shape[0]
    plane, y, core = place()
    chip = 2 * plane + y
    position = (2 * chip + core) * rows + lax.broadcasted_iota(jnp.int32, (rows, rows), 0)
    start = start_ref[...]
    first_start = jnp.min(start[:8])

    if last:
        out_hbm, out_ref, sems = rest

        def emit(at, acc, top, total):
            out_ref[:, at] = (acc / total).astype(jnp.bfloat16)
    else:

        def emit(at, *new):
            rest[0][:, at], rest[1][:, at], rest[2][:, at] = new

    def out_copy(j):
        at = head_columns(j * (GROUP // 2), GROUP // 2)
        return pltpu.make_async_copy(out_ref.at[:, at], out_hbm.at[:, at], sems.at[j])

    def update(used):
        if used:
            keys = [position_in(2 * (chip - places[b][0]) + (core ^ places[b][1]), rows) for b in used]
            bias = [jnp.where((key >= start) & (key <= position), 0.0, NEG) for key in keys]
            bias = jnp.concatenate(bias, axis=1)
        for j in range(KV_HEADS):
            if used:
                key_tile, value_tile = (
                    jnp.concatenate([kv_refs[b][:, head_columns(head)] for b in used], axis=0)
                    for head in (j, KV_HEADS + j)
                )
                update_heads(j, q_ref, key_tile, value_tile, bias, state, emit)
            else:
                for g in range(GROUP):
                    at = head_columns(j * GROUP + g)
                    emit(at, *(x[:, at] for x in state))
            if last:
                out_copy(2 * j).start()
                out_copy(2 * j + 1).start()

    every = list(range(n_blocks))
    nearest, furthest = (pick(offset for offset, _ in places) for pick in (min, max))
    near = [b for b in every if places[b][0] < furthest]

    def seen(offset):
        return (2 * (chip - offset) + 2) * rows > first_start

    pl.when(jnp.logical_not(seen(nearest)))(lambda: update([]))
    if near and len(near) % 2 == 0:
        pl.when(seen(nearest) & jnp.logical_not(seen(furthest)))(lambda: update(near))
        pl.when(seen(furthest))(lambda: update(every))
    else:
        pl.when(seen(nearest))(lambda: update(every))

    if last:
        for j in range(2 * KV_HEADS):
            out_copy(j).wait()


def attend_next(start, queries, blocks, places, state, last=False):
    rows = queries.shape[0]
    wide = jax.ShapeDtypeStruct(queries.shape, jnp.float32)
    scratch = []
    if last:
        scratch = [pltpu.VMEM(queries.shape, queries.dtype), pltpu.SemaphoreType.DMA((2 * KV_HEADS,))]
    return pl.pallas_call(
        functools.partial(next_kernel, last, places),
        out_shape=jax.ShapeDtypeStruct(queries.shape, queries.dtype) if last else (wide,) * 3,
        in_specs=[VMEM] * (2 + len(blocks) + 3),
        out_specs=HBM if last else (VMEM,) * 3,
        scratch_shapes=scratch,
        compiler_params=pltpu.CompilerParams(vmem_limit_bytes=20 * 1024 * 1024),
        cost_estimate=cost(rows, len(blocks)),
    )(start, queries, *blocks, *state)


def cost(rows, blocks):
    keys = rows * blocks
    return pl.CostEstimate(
        flops=4 * rows * HEADS * HEAD_DIM * keys * 10,
        bytes_accessed=rows * HEADS * HEAD_DIM * 8,
        transcendentals=rows * HEADS * keys,
    )


def local(n, queries, keys, values, doc_lengths):
    reach = n // 2 // 4

    def permute(block, target):
        return lax.ppermute(block, "ctx", [(i, target(i)) for i in range(n)])

    def swap(block, bit):
        return permute(block, lambda i: i ^ bit)

    def onward(block, step, hop):
        fixed = 4 * (hop - 1) - 2 * (step % 4)
        return permute(block, lambda i: i ^ 1 if i < fixed else fixed + (i - fixed + step) % (n - fixed))

    def after(block, other):
        return lax.optimization_barrier((block, other))[0]

    def pair(block):
        return block, swap(block, 1)

    own = pack(keys, values)
    beside = swap(own, 2)
    back = onward(own, 4, 1)
    back_beside = lax.ppermute(beside, "ctx", [(i, i + 4) for i in range(n - 4) if i // 2 % 2 == 0])
    far = (onward(after(back, swap(beside, 1)), 4, 2), onward(back, 2, 2)) if reach > 1 else ()
    *state, q, start = attend_first(doc_lengths, queries, *pair(own), *pair(back))
    back_beside, beside, far = after((back_beside, beside, far), state[0])
    even = lax.axis_index("ctx") // 2 % 2 == 0
    across = jnp.where(even, back_beside, beside)
    blocks, places = (across,), (1,)
    for z in range(2, reach + 1):
        here, there = far
        if z < reach:
            far = after((onward(here, 4, z + 1), onward(here, 2, z + 1)), state[0])
        blocks, places = (there,) + blocks, (2 * z - 1,) + places
        other = tuple(swap(block, 1) for block in blocks)
        if len(blocks) == 2:
            state = attend_next(start, q, blocks, tuple((offset, 0) for offset in places), state)
            blocks, places = (), ()
        blocks = blocks + other + pair(here)
        places = tuple((offset, 0) for offset in places) + tuple((offset, 1) for offset in (2 * z - 1, 1)[: len(other)])
        places = places + ((2 * z, 0), (2 * z, 1))
        if z < reach:
            state = attend_next(start, q, blocks, places, state)
            blocks, places = (), ()
    return attend_next(start, q, blocks, places, state, last=True)


def solution(mesh):
    spec = P(("groups", "ctx"), None)
    return jax.shard_map(
        functools.partial(local, mesh.shape["ctx"]),
        mesh=mesh,
        in_specs=(spec, spec, spec, P("groups")),
        out_specs=spec,
        check_vma=False,
    )
```
